256 devices in a mesh: seq: 32 (over z_hi, x, y), ch: 8 (over z_lo, core).
Axes of the slice: x: 4, y: 4, z: 8 (z_hi: 2, z_lo: 4; z = z_hi * 4 + z_lo), core: 2. Of those that a mesh axis runs over, the one named last changes fastest.
Arguments:
- seq_values: bfloat16 [1024, 512, 512], P('ch', 'seq'), may hold values from -6 to 6
- gate_values: bfloat16 [1024, 512, 512], P('ch', 'seq'), may hold values from -6 to 6
- out_grad: bfloat16 [1024, 512, 512], P('ch', 'seq'), may hold values from -6 to 6
- factor_one: bfloat16 [512, 512], replicated, may hold values from -0.25 to 0.25
- factor_two: bfloat16 [512, 512], replicated, may hold values from -0.25 to 0.25
- twiddle: bfloat16 [512, 512], P('seq'), may hold values from 0.3984375 to 1.59375
Outputs:
- values_grad: bfloat16 [1024, 512, 512], P('ch', 'seq')
- gate_grad: bfloat16 [1024, 512, 512], P('ch', 'seq')
- factor_one_grad: float32 [512, 512], P('seq')
- factor_two_grad: float32 [512, 512], P('seq')
- twiddle_grad: float32 [512, 512], P('seq')
The draws below stay inside these ranges and needn't reach their ends.
All inputs are finite; a program needn't handle non-finite values.
Results may differ from the reference program's by a relative error of at most 0.0064.
Values may be sent and summed in bfloat16 or wider, within the bound.
A program may use at most 64 MiB of HBM per device.

```python
import jax
import jax.numpy as jnp
from jax import lax

D = 1024
B = 512
S = 512


def block_scale(own_key, dims, split, smallest, top_value):
    level, own = 1.0, jax.random.fold_in(own_key, 6)
    for axis_at, shards_of in split:
        draws = jnp.exp(jax.random.uniform(jax.random.fold_in(own, axis_at), (shards_of,), jnp.float32, smallest / len(split), top_value / len(split)))
        level = level * jnp.repeat(draws, dims[axis_at] // shards_of).reshape([-1 if axis == axis_at else 1 for axis in range(len(dims))])
    return level


def normal_values(stream_key, shape, spread, limit, pieces=(), dtype=jnp.bfloat16):
    result = spread * jax.random.normal(stream_key, shape, jnp.float32)
    if pieces:
        result = result * block_scale(stream_key, shape, pieces, -0.22, 0.18)
    return jnp.clip(result, -limit, limit).astype(dtype)


def setup_inputs(seed: int = 0) -> dict:
    seeds = jax.random.split(jax.random.key(seed), 7)
    return {
        "seq_values": normal_values(seeds[0], (D, B, S), 1.0, 6.0, ((0, 8), (1, 32))),
        "gate_values": normal_values(seeds[1], (D, B, S), 1.0, 6.0, ((0, 8), (1, 32))),
        "out_grad": normal_values(seeds[2], (D, B, S), 1.0, 6.0, ((0, 8), (1, 32))),
        "factor_one": normal_values(seeds[3], (S, S), S ** -0.5, 0.25),
        "factor_two": normal_values(seeds[4], (B, B), B ** -0.5, 0.25),
        "twiddle": jnp.clip(0.3984375 + 1.1953125 * jax.random.uniform(seeds[5], (B, S), jnp.float32) ** block_scale(seeds[5], (B, S), ((0, 32),), -0.2, 0.2), 0.3984375, 1.59375).astype(jnp.bfloat16),
    }


def reference(seq_values, gate_values, out_grad, factor_one, factor_two, twiddle):
    group = 16
    f32 = jnp.float32
    first = factor_one.astype(f32)
    second = factor_two.astype(f32)
    twiddle_f = twiddle.astype(f32)
    shape = (D // group, group, B, S)
    stacked = (seq_values.reshape(shape), gate_values.reshape(shape), out_grad.reshape(shape))

    def step(carry, items):
        first_sum, second_sum, twiddle_sum = carry
        values, gates, grads = items
        values_f = values.astype(f32)
        pre_twiddle = jnp.einsum('cbs,rs->cbr', values_f, first)
        mixed_first = (pre_twiddle * twiddle_f[None]).astype(jnp.bfloat16)
        mixed = jnp.einsum('cbr,jb->cjr', mixed_first.astype(f32), second).astype(jnp.bfloat16)
        gate_grad = (grads.astype(f32) * mixed.astype(f32)).astype(jnp.bfloat16)
        mixed_grad = (gates.astype(f32) * grads.astype(f32)).astype(jnp.bfloat16)
        mixed_grad_f = mixed_grad.astype(f32)
        first_grad = jnp.einsum('cjr,jb->cbr', mixed_grad_f, second).astype(jnp.bfloat16)
        second_sum = second_sum + jnp.einsum('cjr,cbr->jb', mixed_grad_f, mixed_first.astype(f32))
        first_grad_f = first_grad.astype(f32)
        scaled_grad = (first_grad_f * twiddle_f[None]).astype(jnp.bfloat16)
        twiddle_sum = twiddle_sum + jnp.sum(first_grad_f * pre_twiddle, axis=0)
        scaled_f = scaled_grad.astype(f32)
        values_grad = jnp.einsum('cbr,rs->cbs', scaled_f, first).astype(jnp.bfloat16)
        first_sum = first_sum + jnp.einsum('cbr,cbs->rs', scaled_f, values_f)
        return (first_sum, second_sum, twiddle_sum), (values_grad, gate_grad)

    init = (jnp.zeros((S, S), f32), jnp.zeros((B, B), f32), jnp.zeros((B, S), f32))
    sums, grads_out = lax.scan(step, init, stacked)
    first_sum, second_sum, twiddle_sum = sums
    values_grad = grads_out[0].reshape(D, B, S)
    gate_grad = grads_out[1].reshape(D, B, S)
    factor_one_grad = first_sum * (1.0 / (D * B) ** 0.5)
    factor_two_grad = second_sum * (1.0 / (D * S) ** 0.5)
    twiddle_grad = twiddle_sum * (1.0 / D ** 0.5)
    return (values_grad, gate_grad, factor_one_grad, factor_two_grad, twiddle_grad)
```

```python
import functools

import jax
import jax.numpy as jnp
from jax import lax
from jax.experimental import pallas as pl
from jax.experimental.pallas import tpu as pltpu
from jax.sharding import PartitionSpec as P

MESH = pl.DeviceIdType.MESH
NX, NY, ZH, ZL, NC = 4, 4, 2, 4, 2
PLANE = NX * NY
NZ = ZH * ZL
SEQ = ZH * PLANE
STEPS = 4
MG, MF, FG, MX = 0, STEPS, 2 * STEPS, 3 * STEPS
F32 = jnp.float32
BF16 = jnp.bfloat16


def dot(a, b, ca, cb):
    return lax.dot_general(a, b, (((ca,), (cb,)), ((), ())), preferred_element_type=F32)


def kernel(
    scales,
    x_hbm, gate_hbm, og_hbm, one_hbm, two_hbm, tw_hbm,
    vg_hbm, gg_hbm, one_out, two_out, tw_out,
    x_v, gate_v, og_v, one_v, two_v, two_t, tw_v, pre_v,
    out_buf, relay_buf, in_buf, vg_v, gg_v,
    grad_v, sib_v, sum_v, plane_v, zsend_v, zrecv_v,
    tw_part, tw_sib, tw_sum, tw_recv, fin_v,
    load_sem, mat_sem, store_sem,
    z_send, z_recv, own_send, fwd_send, in_recv,
    sib_send, sib_recv, pl_send, pl_recv, zz_send, zz_recv,
    tws_send, tws_recv, twz_send, twz_recv, fin_send, fin_recv,
):
    seq = lax.axis_index("seq")
    ch = lax.axis_index("ch")
    hi, at = seq // PLANE, seq % PLANE
    px, py = at // NY, at % NY
    lo, core = ch // NC, ch % NC
    z = hi * ZL + lo
    other_hi = 1 - hi

    def plane_at(d):
        return ((px + d // NY) % NX) * NY + (py + d % NY) % NY

    def plane_dev(to):
        return (hi * PLANE + to, ch)

    across = (other_hi * PLANE + at, ch)
    sibling = (seq, lo * NC + 1 - core)

    def z_dev(to):
        return ((to // ZL) * PLANE + at, (to % ZL) * NC + core)

    def remote(src, dst, ssem, rsem, dev):
        return pltpu.make_async_remote_copy(
            src_ref=src, dst_ref=dst, send_sem=ssem, recv_sem=rsem,
            device_id=dev, device_id_type=MESH,
        )

    def drain(ref, sem):
        pltpu.make_async_copy(ref, ref, sem).wait()

    def load(n, src, dst, k):
        return pltpu.make_async_copy(src.at[:, k], dst.at[k], load_sem.at[n, k])

    mats = (
        pltpu.make_async_copy(one_hbm, one_v, mat_sem.at[0]),
        pltpu.make_async_copy(tw_hbm, tw_v, mat_sem.at[1]),
        pltpu.make_async_copy(two_hbm, two_v, mat_sem.at[2]),
    )

    for k in range(STEPS):
        load(0, gate_hbm, gate_v, k).start()
        load(1, og_hbm, og_v, k).start()
    mats[0].start()
    mats[1].start()
    for k in range(STEPS):
        load(2, x_hbm, x_v, k).start()
    mats[2].start()

    barrier = pltpu.get_barrier_semaphore()

    @pl.loop(1, PLANE)
    def _(d):
        pl.semaphore_signal(barrier, inc=1, device_id=plane_dev(plane_at(d)), device_id_type=MESH)

    @pl.loop(1, NZ)
    def _(d):
        pl.semaphore_signal(barrier, inc=1, device_id=z_dev((z + d) % NZ), device_id_type=MESH)

    pl.semaphore_signal(barrier, inc=1, device_id=sibling, device_id_type=MESH)
    pl.semaphore_wait(barrier, PLANE - 1 + NZ - 1 + 1)

    def across_copy(i):
        return remote(
            out_buf.at[i, pl.ds(other_hi * PLANE, PLANE)], relay_buf.at[i],
            z_send.at[i], z_recv.at[i], across,
        )

    def send(i):
        across_copy(i).start()

        @pl.loop(1, PLANE)
        def _(d):
            to = plane_at(d)
            remote(
                out_buf.at[i, hi * PLANE + to], in_buf.at[i, seq],
                own_send.at[i], in_recv.at[i], plane_dev(to),
            ).start()

        pltpu.make_async_copy(out_buf.at[i, seq], in_buf.at[i, seq], in_recv.at[i]).start()

    def forward(i):
        across_copy(i).wait_recv()
        origin = other_hi * PLANE + at

        @pl.loop(1, PLANE)
        def _(d):
            to = plane_at(d)
            remote(
                relay_buf.at[i, to], in_buf.at[i, origin],
                fwd_send.at[i], in_recv.at[i], plane_dev(to),
            ).start()

        pltpu.make_async_copy(relay_buf.at[i, at], in_buf.at[i, origin], in_recv.at[i]).start()

    def arrived(i):
        drain(in_buf.at[i], in_recv.at[i])

    def flat(ref):
        return ref.reshape(SEQ * 16, 512)

    def blocks(value):
        return value.reshape(SEQ, 16, 512)

    @pl.loop(0, STEPS)
    def _(k):
        load(0, gate_hbm, gate_v, k).wait()
        load(1, og_hbm, og_v, k).wait()
        out_buf[MG + k] = (gate_v[k].astype(F32) * og_v[k].astype(F32)).astype(BF16)
        send(MG + k)

    mats[0].wait()
    mats[1].wait()

    @pl.loop(0, STEPS)
    def _(k):
        load(2, x_hbm, x_v, k).wait()
        pre = dot(x_v[k].reshape(SEQ * 16, 512), one_v[...], 1, 1)
        pre_v[k] = blocks(pre)
        out_buf[MF + k] = (blocks(pre) * tw_v[...].astype(F32)[None]).astype(BF16)
        send(MF + k)

    mats[2].wait()
    two_t[...] = two_v[...].T
    grad_v[...] = jnp.zeros_like(grad_v)
    tw_part[...] = jnp.zeros_like(tw_part)
    forward(MG)

    @pl.loop(0, STEPS)
    def _(k):
        forward(MG + k + 1)
        arrived(MG + k)
        grad = in_buf[MG + k].reshape(SEQ * 16, 512)
        out_buf[FG + k] = blocks(dot(two_t[...], grad, 1, 0).astype(BF16))
        send(FG + k)

    @pl.loop(0, STEPS)
    def _(k):
        forward(MF + k + 1)
        arrived(MF + k)
        first = in_buf[MF + k].reshape(SEQ * 16, 512)
        out_buf[MX + k] = blocks(dot(two_v[...], first, 1, 0).astype(BF16))
        send(MX + k)
        part = dot(in_buf[MG + k].reshape(SEQ * 16, 512), first, 1, 1)
        grad_v[0, 0] += part[:, :256].reshape(ZH, PLANE, 16, 256)
        grad_v[0, 1] += part[:, 256:].reshape(ZH, PLANE, 16, 256)

    def pair_copy(m):
        return remote(grad_v.at[m, 1 - core], sib_v.at[m], sib_send.at[m], sib_recv.at[m], sibling)

    def plane_sends(m):
        pair_copy(m).wait_recv()
        sum_v[m] = grad_v[m, core] + sib_v[m]

        @pl.loop(1, PLANE)
        def _(d):
            to = plane_at(d)
            remote(
                sum_v.at[m, :, to], plane_v.at[m, at],
                pl_send.at[m], pl_recv.at[m], plane_dev(to),
            ).start()

        pltpu.make_async_copy(sum_v.at[m, :, at], plane_v.at[m, at], pl_recv.at[m]).start()

    def z_sends(m):
        drain(plane_v.at[m], pl_recv.at[m])
        zsend_v[m] = jnp.sum(plane_v[m], axis=0)

        @pl.loop(1, NZ)
        def _(d):
            to = (z + d) % NZ
            remote(
                zsend_v.at[m, to // ZL], zrecv_v.at[m, z],
                zz_send.at[m], zz_recv.at[m], z_dev(to),
            ).start()

        pltpu.make_async_copy(zsend_v.at[m, hi], zrecv_v.at[m, z], zz_recv.at[m]).start()

    def fin_copy(m):
        return remote(fin_v.at[m, core], fin_v.at[m, core], fin_send.at[m], fin_recv.at[m], sibling)

    def fin_other(m):
        return remote(
            fin_v.at[m, 1 - core], fin_v.at[m, 1 - core], fin_send.at[m], fin_recv.at[m], sibling
        )

    def finish(m):
        drain(zrecv_v.at[m], zz_recv.at[m])
        fin_v[m, core] = jnp.sum(zrecv_v[m], axis=0) * scales[m]
        fin_copy(m).start()

    pair_copy(0).start()
    plane_sends(0)

    def store(n, src, dst, k):
        return pltpu.make_async_copy(src.at[k], dst.at[:, k], store_sem.at[n, k])

    @pl.loop(0, STEPS)
    def _(k):
        forward(FG + k + 1)
        arrived(FG + k)
        fg = in_buf[FG + k].astype(F32)
        scaled = (fg * tw_v[...].astype(F32)[None]).astype(BF16)
        tw_add = jnp.sum(fg * pre_v[k], axis=0)
        tw_part[0] += tw_add[:, :256]
        tw_part[1] += tw_add[:, 256:]
        scaled = scaled.reshape(SEQ * 16, 512)
        vg_v[k] = blocks(dot(scaled, one_v[...], 1, 0).astype(BF16))
        store(0, vg_v, vg_hbm, k).start()
        part = dot(scaled, x_v[k].reshape(SEQ * 16, 512), 0, 0)
        grad_v[1, 0] += part[:, :256].reshape(ZH, PLANE, 16, 256)
        grad_v[1, 1] += part[:, 256:].reshape(ZH, PLANE, 16, 256)

    def tw_pair():
        return remote(tw_part.at[1 - core], tw_sib, tws_send, tws_recv, sibling)

    pair_copy(1).start()
    tw_pair().start()
    z_sends(0)
    plane_sends(1)
    tw_pair().wait_recv()
    tw_sum[...] = tw_part[core] + tw_sib[...]

    @pl.loop(1, ZL)
    def _(d):
        to = (lo + d) % ZL
        remote(
            tw_sum, tw_recv.at[lo], twz_send, twz_recv, (seq, to * NC + core)
        ).start()

    pltpu.make_async_copy(tw_sum, tw_recv.at[lo], twz_recv).start()
    z_sends(1)

    def gate(k):
        arrived(MX + k)
        gg_v[k] = (og_v[k].astype(F32) * in_buf[MX + k].astype(F32)).astype(BF16)
        store(1, gg_v, gg_hbm, k).start()

    @pl.loop(0, STEPS - 1)
    def _(k):
        forward(MX + k + 1)
        gate(k)

    finish(0)
    drain(tw_recv, twz_recv)
    fin_v[2, core] = jnp.sum(tw_recv[...], axis=0) * scales[2]
    fin_copy(2).start()
    finish(1)
    gate(STEPS - 1)

    for m, out in ((0, two_out), (2, tw_out), (1, one_out)):
        fin_other(m).wait_recv()
        out[:, :256] = fin_v[m, 0]
        out[:, 256:] = fin_v[m, 1]

    for k in range(STEPS):
        store(0, vg_v, vg_hbm, k).wait()
        store(1, gg_v, gg_hbm, k).wait()

    @pl.loop(0, 4 * STEPS)
    def _(i):
        across_copy(i).wait_send()
        drain(in_buf.at[i, pl.ds(0, PLANE - 1)], own_send.at[i])
        drain(in_buf.at[i, pl.ds(0, PLANE - 1)], fwd_send.at[i])

    for m in range(2):
        pair_copy(m).wait_send()
        drain(plane_v.at[m, pl.ds(0, PLANE - 1)], pl_send.at[m])
        drain(zrecv_v.at[m, pl.ds(0, NZ - 1)], zz_send.at[m])
    tw_pair().wait_send()
    drain(tw_recv.at[pl.ds(0, ZL - 1)], twz_send)
    for m in range(3):
        fin_copy(m).wait_send()


def body(seq_values, gate_values, out_grad, factor_one, factor_two, twiddle):
    width = seq_values.shape[0] * ZL * NC
    nblocks = factor_two.shape[0]
    block_len = factor_one.shape[0]
    scales = (
        1.0 / (width * block_len) ** 0.5,
        1.0 / (width * nblocks) ** 0.5,
        1.0 / width**0.5,
    )
    shape = (SEQ, STEPS, 16, 512)
    big = jax.ShapeDtypeStruct(shape, BF16)
    rows = jax.ShapeDtypeStruct((16, 512), F32)
    anywhere = pl.BlockSpec(memory_space=pl.ANY)
    vmem = pl.BlockSpec(memory_space=pltpu.VMEM)
    per_step = (STEPS, SEQ, 16, 512)
    dma = pltpu.SemaphoreType.DMA
    items = 4 * STEPS
    vg, gg, one, two, tw = pl.pallas_call(
        functools.partial(kernel, scales),
        out_shape=(big, big, rows, rows, rows),
        in_specs=[anywhere] * 6,
        out_specs=(anywhere, anywhere, vmem, vmem, vmem),
        scratch_shapes=[
            pltpu.VMEM(per_step, BF16),
            pltpu.VMEM(per_step, BF16),
            pltpu.VMEM(per_step, BF16),
            pltpu.VMEM((512, 512), BF16),
            pltpu.VMEM((512, 512), BF16),
            pltpu.VMEM((512, 512), BF16),
            pltpu.VMEM((16, 512), BF16),
            pltpu.VMEM(per_step, F32),
            pltpu.VMEM((items, SEQ, 16, 512), BF16),
            pltpu.VMEM((items, PLANE, 16, 512), BF16),
            pltpu.VMEM((items, SEQ, 16, 512), BF16),
            pltpu.VMEM(per_step, BF16),
            pltpu.VMEM(per_step, BF16),
            pltpu.VMEM((2, 2, ZH, PLANE, 16, 256), F32),
            pltpu.VMEM((2, ZH, PLANE, 16, 256), F32),
            pltpu.VMEM((2, ZH, PLANE, 16, 256), F32),
            pltpu.VMEM((2, PLANE, ZH, 16, 256), F32),
            pltpu.VMEM((2, ZH, 16, 256), F32),
            pltpu.VMEM((2, NZ, 16, 256), F32),
            pltpu.VMEM((2, 16, 256), F32),
            pltpu.VMEM((16, 256), F32),
            pltpu.VMEM((16, 256), F32),
            pltpu.VMEM((ZL, 16, 256), F32),
            pltpu.VMEM((3, 2, 16, 256), F32),
            dma((3, STEPS)), dma((3,)), dma((2, STEPS)),
            dma((items,)), dma((items,)), dma((items,)), dma((items,)), dma((items,)),
            dma((2,)), dma((2,)), dma((2,)), dma((2,)), dma((2,)), dma((2,)),
            dma(()), dma(()), dma(()), dma(()), dma((3,)), dma((3,)),
        ],
        compiler_params=pltpu.CompilerParams(
            collective_id=0, has_side_effects=True, vmem_limit_bytes=60 * 2**20
        ),
    )(
        seq_values.reshape(shape), gate_values.reshape(shape), out_grad.reshape(shape),
        factor_one, factor_two, twiddle,
    )
    whole = seq_values.shape
    return (vg.reshape(whole), gg.reshape(whole), one, two, tw)


def solution(mesh):
    return jax.shard_map(
        body,
        mesh=mesh,
        in_specs=(
            P("ch", "seq", None),
            P("ch", "seq", None),
            P("ch", "seq", None),
            P(),
            P(),
            P("seq", None),
        ),
        out_specs=(
            P("ch", "seq", None),
            P("ch", "seq", None),
            P("seq", None),
            P("seq", None),
            P("seq", None),
        ),
        check_vma=False,
    )
```

```python
import functools

import jax
import jax.numpy as jnp
from jax import lax
from jax.experimental import pallas as pl
from jax.experimental.pallas import tpu as pltpu
from jax.sharding import PartitionSpec as P

MESH = pl.DeviceIdType.MESH
NX, NY, ZH, ZL, NC = 4, 4, 2, 4, 2
PLANE = NX * NY
NZ = ZH * ZL
SEQ = ZH * PLANE
STEPS = 4
MG, MF, FG, MX = 0, STEPS, 2 * STEPS, 3 * STEPS
F32 = jnp.float32
BF16 = jnp.bfloat16


def dot(a, b, ca, cb):
    return lax.dot_general(a, b, (((ca,), (cb,)), ((), ())), preferred_element_type=F32)


def kernel(
    scales,
    x_hbm, gate_hbm, og_hbm, one_hbm, two_hbm, tw_hbm,
    vg_out, gg_out, fin_out,
    x_v, gate_v, og_v, one_v, two_v, two_t, tw_v, pre_v,
    out_buf, relay_buf, in_buf, vg_v, gg_v,
    grad_v, sib_v, sum_v, plane_v, zsend_v, zrecv_v,
    tw_part, tw_sib, tw_sum, tw_recv, fin_v,
    load_sem, mat_sem, store_sem, keep_sem,
    z_send, z_recv, own_send, fwd_send, in_recv, direct_send,
    sib_send, sib_recv, pl_send, pl_recv, zz_send, zz_recv,
    tws_send, tws_recv, twz_send, twz_recv, fin_send, fin_recv,
):
    seq = lax.axis_index("seq")
    ch = lax.axis_index("ch")
    hi, at = seq // PLANE, seq % PLANE
    px, py = at // NY, at % NY
    lo, core = ch // NC, ch % NC
    z = hi * ZL + lo
    other_hi = 1 - hi

    def plane_at(d):
        return ((px + d // NY) % NX) * NY + (py + d % NY) % NY

    def plane_dev(to):
        return (hi * PLANE + to, ch)

    across = (other_hi * PLANE + at, ch)
    sibling = (seq, lo * NC + 1 - core)

    def z_dev(to):
        return ((to // ZL) * PLANE + at, (to % ZL) * NC + core)

    def remote(src, dst, ssem, rsem, dev):
        return pltpu.make_async_remote_copy(
            src_ref=src, dst_ref=dst, send_sem=ssem, recv_sem=rsem,
            device_id=dev, device_id_type=MESH,
        )

    def drain(ref, sem):
        pltpu.make_async_copy(ref, ref, sem).wait()

    def load(n, src, dst, k):
        return pltpu.make_async_copy(src.at[:, k], dst.at[k], load_sem.at[n, k])

    mats = (
        pltpu.make_async_copy(one_hbm, one_v, mat_sem.at[0]),
        pltpu.make_async_copy(tw_hbm, tw_v, mat_sem.at[1]),
        pltpu.make_async_copy(two_hbm, two_v, mat_sem.at[2]),
    )

    for k in range(STEPS):
        load(0, gate_hbm, gate_v, k).start()
        load(1, og_hbm, og_v, k).start()
    mats[0].start()
    mats[1].start()
    for k in range(STEPS):
        load(2, x_hbm, x_v, k).start()
    mats[2].start()

    barrier = pltpu.get_barrier_semaphore()

    @pl.loop(1, PLANE)
    def _(d):
        pl.semaphore_signal(barrier, inc=1, device_id=plane_dev(plane_at(d)), device_id_type=MESH)

    @pl.loop(1, NZ)
    def _(d):
        pl.semaphore_signal(barrier, inc=1, device_id=z_dev((z + d) % NZ), device_id_type=MESH)

    @pl.loop(1, PLANE)
    def _(d):
        to = (other_hi * PLANE + plane_at(d), ch)
        pl.semaphore_signal(barrier, inc=1, device_id=to, device_id_type=MESH)

    pl.semaphore_signal(barrier, inc=1, device_id=sibling, device_id_type=MESH)

    def across_copy(i):
        return remote(
            out_buf.at[i, pl.ds(other_hi * PLANE, PLANE)], relay_buf.at[i],
            z_send.at[i], z_recv.at[i], across,
        )

    def send_across(i):
        across_copy(i).start()

    def send_direct(i):
        @pl.loop(0, PLANE)
        def _(d):
            to = other_hi * PLANE + plane_at(d)
            remote(
                out_buf.at[i, to], in_buf.at[i, seq], direct_send, in_recv.at[i], (to, ch)
            ).start()

    def send_own(i):
        @pl.loop(1, PLANE)
        def _(d):
            to = plane_at(d)
            remote(
                out_buf.at[i, hi * PLANE + to], in_buf.at[i, seq],
                own_send.at[i], in_recv.at[i], plane_dev(to),
            ).start()

        pltpu.make_async_copy(out_buf.at[i, seq], in_buf.at[i, seq], in_recv.at[i]).start()

    def forward(i):
        across_copy(i).wait_recv()
        origin = other_hi * PLANE + at

        @pl.loop(1, PLANE)
        def _(d):
            to = plane_at(d)
            remote(
                relay_buf.at[i, to], in_buf.at[i, origin],
                fwd_send.at[i], in_recv.at[i], plane_dev(to),
            ).start()

        pltpu.make_async_copy(relay_buf.at[i, at], in_buf.at[i, origin], in_recv.at[i]).start()

    def arrived(i):
        drain(in_buf.at[i], in_recv.at[i])

    def flat(ref):
        return ref.reshape(SEQ * 16, 512)

    def blocks(value):
        return value.reshape(SEQ, 16, 512)

    @pl.loop(0, STEPS)
    def _(k):
        load(0, gate_hbm, gate_v, k).wait()
        load(1, og_hbm, og_v, k).wait()
        out_buf[MG + k] = (gate_v[k].astype(F32) * og_v[k].astype(F32)).astype(BF16)

    pl.semaphore_wait(barrier, 2 * (PLANE - 1) + NZ - 1 + 1)

    @pl.loop(MG, MG + STEPS)
    def _(i):
        send_across(i)

    @pl.loop(MG, MG + STEPS)
    def _(i):
        send_own(i)

    mats[0].wait()
    mats[1].wait()

    @pl.loop(0, STEPS)
    def _(k):
        load(2, x_hbm, x_v, k).wait()
        pre = dot(x_v[k].reshape(SEQ * 16, 512), one_v[...], 1, 1)
        pre_v[k] = blocks(pre)
        out_buf[MF + k] = (blocks(pre) * tw_v[...].astype(F32)[None]).astype(BF16)
        send_across(MF + k)
        send_own(MF + k)

    mats[2].wait()
    two_t[...] = two_v[...].T
    grad_v[...] = jnp.zeros_like(grad_v)
    tw_part[...] = jnp.zeros_like(tw_part)
    forward(MG)

    @pl.loop(0, STEPS)
    def _(k):
        forward(MG + k + 1)
        arrived(MG + k)
        grad = in_buf[MG + k].reshape(SEQ * 16, 512)
        out_buf[FG + k] = blocks(dot(two_t[...], grad, 1, 0).astype(BF16))
        send_across(FG + k)
        send_own(FG + k)

    @pl.loop(0, STEPS)
    def _(k):
        forward(MF + k + 1)
        arrived(MF + k)
        first = in_buf[MF + k].reshape(SEQ * 16, 512)
        out_buf[MX + k] = blocks(dot(two_v[...], first, 1, 0).astype(BF16))

        @pl.when(k < STEPS - 1)
        def _():
            send_across(MX + k)

        send_own(MX + k)
        part = dot(in_buf[MG + k].reshape(SEQ * 16, 512), first, 1, 1)
        grad_v[0, 0] += part[:, :256].reshape(ZH, PLANE, 16, 256)
        grad_v[0, 1] += part[:, 256:].reshape(ZH, PLANE, 16, 256)

    def pair_copy(m):
        return remote(grad_v.at[m, 1 - core], sib_v.at[m], sib_send.at[m], sib_recv.at[m], sibling)

    def plane_sends(m):
        pair_copy(m).wait_recv()
        sum_v[m] = grad_v[m, core] + sib_v[m]

        @pl.loop(1, PLANE)
        def _(d):
            to = plane_at(d)
            remote(
                sum_v.at[m, :, to], plane_v.at[m, at],
                pl_send.at[m], pl_recv.at[m], plane_dev(to),
            ).start()

        pltpu.make_async_copy(sum_v.at[m, :, at], plane_v.at[m, at], pl_recv.at[m]).start()

    def z_sends(m):
        drain(plane_v.at[m], pl_recv.at[m])
        zsend_v[m] = jnp.sum(plane_v[m], axis=0).astype(BF16)

        @pl.loop(1, NZ)
        def _(d):
            to = (z + d) % NZ
            remote(
                zsend_v.at[m, to // ZL], zrecv_v.at[m, z],
                zz_send.at[m], zz_recv.at[m], z_dev(to),
            ).start()

        pltpu.make_async_copy(zsend_v.at[m, hi], zrecv_v.at[m, z], zz_recv.at[m]).start()

    def fin_copy(m):
        return remote(fin_v.at[m, core], fin_v.at[m, core], fin_send.at[m], fin_recv.at[m], sibling)

    def fin_other(m):
        return remote(
            fin_v.at[m, 1 - core], fin_v.at[m, 1 - core], fin_send.at[m], fin_recv.at[m], sibling
        )

    def finish(m):
        drain(zrecv_v.at[m], zz_recv.at[m])
        fin_v[m, core] = jnp.sum(zrecv_v[m].astype(F32), axis=0) * scales[m]
        fin_copy(m).start()

    pair_copy(0).start()
    plane_sends(0)

    def store(n, src, dst, k):
        return pltpu.make_async_copy(src.at[k], dst.at[k], store_sem.at[n, k])

    @pl.loop(0, STEPS)
    def _(k):
        forward(FG + k + 1)
        arrived(FG + k)
        fg = in_buf[FG + k].astype(F32)
        scaled = (fg * tw_v[...].astype(F32)[None]).astype(BF16)
        tw_add = jnp.sum(fg * pre_v[k], axis=0)
        tw_part[0] += tw_add[:, :256]
        tw_part[1] += tw_add[:, 256:]
        scaled = scaled.reshape(SEQ * 16, 512)
        vg_v[k] = blocks(dot(scaled, one_v[...], 1, 0).astype(BF16))
        store(0, vg_v, vg_out, k).start()
        part = dot(scaled, x_v[k].reshape(SEQ * 16, 512), 0, 0)
        grad_v[1, 0] += part[:, :256].reshape(ZH, PLANE, 16, 256)
        grad_v[1, 1] += part[:, 256:].reshape(ZH, PLANE, 16, 256)

    def tw_pair():
        return remote(tw_part.at[1 - core], tw_sib, tws_send, tws_recv, sibling)

    pair_copy(1).start()
    tw_pair().start()
    z_sends(0)
    plane_sends(1)
    tw_pair().wait_recv()
    tw_sum[...] = (tw_part[core] + tw_sib[...]).astype(BF16)

    @pl.loop(1, ZL)
    def _(d):
        to = (lo + d) % ZL
        remote(
            tw_sum, tw_recv.at[lo], twz_send, twz_recv, (seq, to * NC + core)
        ).start()

    pltpu.make_async_copy(tw_sum, tw_recv.at[lo], twz_recv).start()
    z_sends(1)
    send_direct(MX + STEPS - 1)

    def gate(k):
        arrived(MX + k)
        gg_v[k] = (og_v[k].astype(F32) * in_buf[MX + k].astype(F32)).astype(BF16)
        store(1, gg_v, gg_out, k).start()

    @pl.loop(0, STEPS - 2)
    def _(k):
        forward(MX + k + 1)
        gate(k)

    gate(STEPS - 2)

    finish(0)
    drain(tw_recv, twz_recv)
    fin_v[2, core] = jnp.sum(tw_recv[...].astype(F32), axis=0) * scales[2]
    fin_copy(2).start()
    finish(1)
    gate(STEPS - 1)

    for m in range(3):
        fin_other(m).wait_recv()
    keep = pltpu.make_async_copy(fin_v, fin_out, keep_sem)
    keep.start()
    keep.wait()

    for k in range(STEPS):
        store(0, vg_v, vg_out, k).wait()
        store(1, gg_v, gg_out, k).wait()

    @pl.loop(0, 4 * STEPS - 1)
    def _(i):
        across_copy(i).wait_send()
        drain(in_buf.at[i, pl.ds(0, PLANE - 1)], own_send.at[i])
        drain(in_buf.at[i, pl.ds(0, PLANE - 1)], fwd_send.at[i])

    last = 4 * STEPS - 1
    drain(in_buf.at[last, pl.ds(0, PLANE - 1)], own_send.at[last])
    drain(in_buf.at[last, pl.ds(0, PLANE)], direct_send)

    for m in range(2):
        pair_copy(m).wait_send()
        drain(plane_v.at[m, pl.ds(0, PLANE - 1)], pl_send.at[m])
        drain(zrecv_v.at[m, pl.ds(0, NZ - 1)], zz_send.at[m])
    tw_pair().wait_send()
    drain(tw_recv.at[pl.ds(0, ZL - 1)], twz_send)
    for m in range(3):
        fin_copy(m).wait_send()


def write_out(vg_in, gg_in, fin_in, vg, gg, two, one, tw, big_sem, fin_sem):
    copies = [
        pltpu.make_async_copy(src.at[k], dst.at[:, k], big_sem.at[n, k])
        for k in range(STEPS)
        for n, (src, dst) in enumerate(((vg_in, vg), (gg_in, gg)))
    ]
    copies += [
        pltpu.make_async_copy(
            fin_in.at[m, half], dst.at[:, pl.ds(half * 256, 256)], fin_sem.at[m, half]
        )
        for half in range(2)
        for m, dst in enumerate((two, one, tw))
    ]
    for copy in copies:
        copy.start()
    for copy in copies:
        copy.wait()


def body(seq_values, gate_values, out_grad, factor_one, factor_two, twiddle):
    width = seq_values.shape[0] * ZL * NC
    nblocks = factor_two.shape[0]
    block_len = factor_one.shape[0]
    scales = (
        1.0 / (width * block_len) ** 0.5,
        1.0 / (width * nblocks) ** 0.5,
        1.0 / width**0.5,
    )
    shape = (SEQ, STEPS, 16, 512)
    big = jax.ShapeDtypeStruct(shape, BF16)
    rows = jax.ShapeDtypeStruct((16, 512), F32)
    anywhere = pl.BlockSpec(memory_space=pl.ANY)
    per_step = (STEPS, SEQ, 16, 512)
    dma = pltpu.SemaphoreType.DMA
    items = 4 * STEPS
    kept = pl.pallas_call(
        functools.partial(kernel, scales),
        out_shape=(
            pltpu.VMEM(per_step, BF16),
            pltpu.VMEM(per_step, BF16),
            pltpu.VMEM((3, 2, 16, 256), F32),
        ),
        in_specs=[anywhere] * 6,
        out_specs=(anywhere,) * 3,
        scratch_shapes=[
            pltpu.VMEM(per_step, BF16),
            pltpu.VMEM(per_step, BF16),
            pltpu.VMEM(per_step, BF16),
            pltpu.VMEM((512, 512), BF16),
            pltpu.VMEM((512, 512), BF16),
            pltpu.VMEM((512, 512), BF16),
            pltpu.VMEM((16, 512), BF16),
            pltpu.VMEM(per_step, F32),
            pltpu.VMEM((items, SEQ, 16, 512), BF16),
            pltpu.VMEM((items - 1, PLANE, 16, 512), BF16),
            pltpu.VMEM((items, SEQ, 16, 512), BF16),
            pltpu.VMEM(per_step, BF16),
            pltpu.VMEM(per_step, BF16),
            pltpu.VMEM((2, 2, ZH, PLANE, 16, 256), F32),
            pltpu.VMEM((2, ZH, PLANE, 16, 256), F32),
            pltpu.VMEM((2, ZH, PLANE, 16, 256), F32),
            pltpu.VMEM((2, PLANE, ZH, 16, 256), F32),
            pltpu.VMEM((2, ZH, 16, 256), BF16),
            pltpu.VMEM((2, NZ, 16, 256), BF16),
            pltpu.VMEM((2, 16, 256), F32),
            pltpu.VMEM((16, 256), F32),
            pltpu.VMEM((16, 256), BF16),
            pltpu.VMEM((ZL, 16, 256), BF16),
            pltpu.VMEM((3, 2, 16, 256), F32),
            dma((3, STEPS)), dma((3,)), dma((2, STEPS)), dma(()),
            dma((items - 1,)), dma((items - 1,)), dma((items,)), dma((items - 1,)), dma((items,)),
            dma(()),
            dma((2,)), dma((2,)), dma((2,)), dma((2,)), dma((2,)), dma((2,)),
            dma(()), dma(()), dma(()), dma(()), dma((3,)), dma((3,)),
        ],
        compiler_params=pltpu.CompilerParams(
            collective_id=0, has_side_effects=True, vmem_limit_bytes=50 * 2**20
        ),
    )(
        seq_values.reshape(shape), gate_values.reshape(shape), out_grad.reshape(shape),
        factor_one, factor_two, twiddle,
    )
    vg, gg, two, one, tw = pl.pallas_call(
        write_out,
        out_shape=(big, big, rows, rows, rows),
        in_specs=[anywhere] * 3,
        out_specs=(anywhere,) * 5,
        scratch_shapes=[dma((2, STEPS)), dma((3, 2))],
        compiler_params=pltpu.CompilerParams(vmem_limit_bytes=4 * 2**20),
    )(*(pltpu.with_memory_space_constraint(part, pltpu.VMEM) for part in kept))
    whole = seq_values.shape
    return (vg.reshape(whole), gg.reshape(whole), one, two, tw)


def solution(mesh):
    return jax.shard_map(
        body,
        mesh=mesh,
        in_specs=(
            P("ch", "seq", None),
            P("ch", "seq", None),
            P("ch", "seq", None),
            P(),
            P(),
            P("seq", None),
        ),
        out_specs=(
            P("ch", "seq", None),
            P("ch", "seq", None),
            P("seq", None),
            P("seq", None),
            P("seq", None),
        ),
        check_vma=False,
    )
```

```python
import functools

import jax
import jax.numpy as jnp
from jax import lax
from jax.experimental import pallas as pl
from jax.experimental.pallas import tpu as pltpu
from jax.sharding import PartitionSpec as P

MESH = pl.DeviceIdType.MESH
NX, NY, ZH, ZL, NC = 4, 4, 2, 4, 2
PLANE = NX * NY
NZ = ZH * ZL
SEQ = ZH * PLANE
STEPS = 4
PARTS = 4
MG, MF, FG, MX = 0, STEPS, 2 * STEPS, 3 * STEPS
F32 = jnp.float32
BF16 = jnp.bfloat16


def dot(a, b, ca, cb):
    return lax.dot_general(a, b, (((ca,), (cb,)), ((), ())), preferred_element_type=F32)


def kernel(
    scales,
    x_hbm, gate_hbm, og_hbm, one_hbm, two_hbm, tw_hbm,
    vg_out, gg_out, fin_out,
    x_v, gate_v, og_v, one_v, two_v, two_t, tw_v, pre_v,
    out_buf, relay_buf, in_buf,
    grad_v, sib_v, sum_v, plane_v, zsend_v, zrecv_v,
    tw_part, tw_sib, tw_sum, tw_recv, fin_v,
    load_sem, mat_sem, round_sem, go_sem,
    z_send, z_recv, own_send, fwd_send, in_recv, direct_send,
    sib_send, sib_recv, pl_send, pl_recv, zz_send, zz_recv,
    tws_send, tws_recv, twz_send, twz_recv, fin_send, fin_recv,
):
    seq = lax.axis_index("seq")
    ch = lax.axis_index("ch")
    hi, at = seq // PLANE, seq % PLANE
    px, py = at // NY, at % NY
    lo, core = ch // NC, ch % NC
    z = hi * ZL + lo
    other_hi = 1 - hi

    def plane_at(d):
        return ((px + d // NY) % NX) * NY + (py + d % NY) % NY

    def plane_dev(to):
        return (hi * PLANE + to, ch)

    across = (other_hi * PLANE + at, ch)
    sibling = (seq, lo * NC + 1 - core)

    def z_dev(to):
        return ((to // ZL) * PLANE + at, (to % ZL) * NC + core)

    def remote(src, dst, ssem, rsem, dev):
        return pltpu.make_async_remote_copy(
            src_ref=src, dst_ref=dst, send_sem=ssem, recv_sem=rsem,
            device_id=dev, device_id_type=MESH,
        )

    def drain(ref, sem):
        pltpu.make_async_copy(ref, ref, sem).wait()

    def load(n, src, dst, k):
        return pltpu.make_async_copy(src.at[:, k], dst.at[k], load_sem.at[n, k])

    mats = (
        pltpu.make_async_copy(one_hbm, one_v, mat_sem.at[0]),
        pltpu.make_async_copy(tw_hbm, tw_v, mat_sem.at[1]),
        pltpu.make_async_copy(two_hbm, two_v, mat_sem.at[2]),
    )

    load(0, gate_hbm, gate_v, 0).start()
    load(1, og_hbm, og_v, 0).start()

    is_hub = (px % 2 == lo // 2) & (py % 2 == lo % 2) & (core == 0)

    def hub_at(h, bx, by, l):
        return (h * PLANE + (2 * bx + l // 2) * NY + 2 * by + l % 2, l * NC)

    bx, by = px // 2, py // 2
    my_hub = hub_at(hi, bx, by, lo)
    edges = (
        hub_at(hi, 1 - bx, by, lo),
        hub_at(hi, bx, 1 - by, lo),
        hub_at(hi, bx, by, lo + 1 - 2 * (lo % 2)),
        hub_at(hi, bx, by, (lo + 2) % ZL),
        across,
    )

    def member(j):
        mx = 2 * bx + (lo // 2 + j // 4) % 2
        my = 2 * by + (lo + j // 2) % 2
        return (hi * PLANE + mx * NY + my, lo * NC + j % 2)

    def tell(sem, dev):
        pl.semaphore_signal(sem, inc=1, device_id=dev, device_id_type=MESH)

    barrier = pltpu.get_barrier_semaphore()
    tell(barrier, across)

    @pl.when(is_hub)
    def _():
        for dev in edges[:-1]:
            tell(barrier, dev)

        @pl.loop(1, 8)
        def _(j):
            tell(barrier, member(j))

    @pl.when(jnp.logical_not(is_hub))
    def _():
        tell(barrier, my_hub)

    def enter():
        @pl.when(is_hub)
        def _():
            pl.semaphore_wait(barrier, 1 + len(edges) - 1 + 7)

        @pl.when(jnp.logical_not(is_hub))
        def _():
            pl.semaphore_wait(barrier, 2)

    def everyone_in():
        @pl.when(is_hub)
        def _():
            for n, dev in enumerate(edges):
                tell(round_sem.at[n], dev)
                pl.semaphore_wait(round_sem.at[n], 1)

            @pl.loop(1, 8)
            def _(j):
                tell(go_sem, member(j))

        @pl.when(jnp.logical_not(is_hub))
        def _():
            pl.semaphore_wait(go_sem, 1)

    for k in range(1, STEPS):
        load(0, gate_hbm, gate_v, k).start()
        load(1, og_hbm, og_v, k).start()
    mats[0].start()
    mats[1].start()
    for k in range(STEPS):
        load(2, x_hbm, x_v, k).start()
    mats[2].start()


    def across_copy(i):
        return remote(
            out_buf.at[i, pl.ds(other_hi * PLANE, PLANE)], relay_buf.at[i],
            z_send.at[i], z_recv.at[i], across,
        )

    def send_across(i):
        across_copy(i).start()

    def send_direct(i):
        @pl.loop(0, PLANE)
        def _(d):
            to = other_hi * PLANE + plane_at(d)
            remote(
                out_buf.at[i, to], in_buf.at[i, seq], direct_send, in_recv.at[i], (to, ch)
            ).start()

    def send_own(i):
        @pl.loop(1, PLANE)
        def _(d):
            to = plane_at(d)
            remote(
                out_buf.at[i, hi * PLANE + to], in_buf.at[i, seq],
                own_send.at[i], in_recv.at[i], plane_dev(to),
            ).start()

        pltpu.make_async_copy(out_buf.at[i, seq], in_buf.at[i, seq], in_recv.at[i]).start()

    def forward(i):
        across_copy(i).wait_recv()
        origin = other_hi * PLANE + at

        @pl.loop(1, PLANE)
        def _(d):
            to = plane_at(d)
            remote(
                relay_buf.at[i, to], in_buf.at[i, origin],
                fwd_send.at[i], in_recv.at[i], plane_dev(to),
            ).start()

        pltpu.make_async_copy(relay_buf.at[i, at], in_buf.at[i, origin], in_recv.at[i]).start()

    def arrived(i):
        drain(in_buf.at[i], in_recv.at[i])

    def flat(ref):
        return ref.reshape(SEQ * 16, 512)

    def blocks(value):
        return value.reshape(SEQ, 16, 512)

    def grad_at_home(k):
        load(0, gate_hbm, gate_v, k).wait()
        load(1, og_hbm, og_v, k).wait()
        out_buf[MG + k] = (gate_v[k].astype(F32) * og_v[k].astype(F32)).astype(BF16)

    grad_at_home(0)
    enter()
    send_across(MG)

    @pl.loop(1, STEPS)
    def _(k):
        grad_at_home(k)
        send_across(MG + k)

    mats[0].wait()
    mats[1].wait()

    @pl.loop(0, STEPS)
    def _(k):
        load(2, x_hbm, x_v, k).wait()
        pre = dot(x_v[k].reshape(SEQ * 16, 512), one_v[...], 1, 1)
        pre_v[k] = blocks(pre)
        out_buf[MF + k] = (blocks(pre) * tw_v[...].astype(F32)[None]).astype(BF16)
        send_across(MF + k)

    everyone_in()

    @pl.loop(MG, MF + STEPS)
    def _(i):
        send_own(i)

    mats[2].wait()
    two_t[...] = two_v[...].T
    grad_v[...] = jnp.zeros_like(grad_v)
    tw_part[...] = jnp.zeros_like(tw_part)
    forward(MG)

    @pl.loop(0, STEPS)
    def _(k):
        forward(MG + k + 1)
        arrived(MG + k)
        grad = in_buf[MG + k].reshape(SEQ * 16, 512)
        out_buf[FG + k] = blocks(dot(two_t[...], grad, 1, 0).astype(BF16))
        send_across(FG + k)
        send_own(FG + k)

    @pl.loop(0, STEPS)
    def _(k):
        forward(MF + k + 1)
        arrived(MF + k)
        first = in_buf[MF + k].reshape(SEQ * 16, 512)
        out_buf[MX + k] = blocks(dot(two_v[...], first, 1, 0).astype(BF16))

        @pl.when(k < STEPS - 1)
        def _():
            send_across(MX + k)

        send_own(MX + k)
        part = dot(in_buf[MG + k].reshape(SEQ * 16, 512), first, 1, 1)
        grad_v[0, 0] += part[:, :256].reshape(ZH, PLANE, 16, 256)
        grad_v[0, 1] += part[:, 256:].reshape(ZH, PLANE, 16, 256)

    def pair_copy(m):
        return remote(grad_v.at[m, 1 - core], sib_v.at[m], sib_send.at[m], sib_recv.at[m], sibling)

    def plane_sends(m):
        pair_copy(m).wait_recv()
        sum_v[m] = grad_v[m, core] + sib_v[m]

        @pl.loop(1, PLANE)
        def _(d):
            to = plane_at(d)
            remote(
                sum_v.at[m, :, to], plane_v.at[m, at],
                pl_send.at[m], pl_recv.at[m], plane_dev(to),
            ).start()

        pltpu.make_async_copy(sum_v.at[m, :, at], plane_v.at[m, at], pl_recv.at[m]).start()

    def z_sends(m):
        drain(plane_v.at[m], pl_recv.at[m])
        zsend_v[m] = jnp.sum(plane_v[m], axis=0).astype(BF16)

        @pl.loop(1, NZ)
        def _(d):
            to = (z + d) % NZ
            remote(
                zsend_v.at[m, to // ZL], zrecv_v.at[m, z],
                zz_send.at[m], zz_recv.at[m], z_dev(to),
            ).start()

        pltpu.make_async_copy(zsend_v.at[m, hi], zrecv_v.at[m, z], zz_recv.at[m]).start()

    def fin_copy(m):
        return remote(fin_v.at[m, core], fin_v.at[m, core], fin_send.at[m], fin_recv.at[m], sibling)

    def fin_other(m):
        return remote(
            fin_v.at[m, 1 - core], fin_v.at[m, 1 - core], fin_send.at[m], fin_recv.at[m], sibling
        )

    def finish(m):
        drain(zrecv_v.at[m], zz_recv.at[m])
        fin_v[m, core] = jnp.sum(zrecv_v[m].astype(F32), axis=0) * scales[m]
        fin_copy(m).start()

    pair_copy(0).start()
    plane_sends(0)

    @pl.loop(0, STEPS)
    def _(k):
        @pl.when(k < STEPS - 1)
        def _():
            forward(FG + k + 1)

        arrived(FG + k)
        fg = in_buf[FG + k].astype(F32)
        scaled = (fg * tw_v[...].astype(F32)[None]).astype(BF16)
        tw_add = jnp.sum(fg * pre_v[k], axis=0)
        tw_part[0] += tw_add[:, :256]
        tw_part[1] += tw_add[:, 256:]
        scaled = scaled.reshape(SEQ * 16, 512)
        vg_out[:, k] = blocks(dot(scaled, one_v[...], 1, 0).astype(BF16))
        part = dot(scaled, x_v[k].reshape(SEQ * 16, 512), 0, 0)
        grad_v[1, 0] += part[:, :256].reshape(ZH, PLANE, 16, 256)
        grad_v[1, 1] += part[:, 256:].reshape(ZH, PLANE, 16, 256)

    def tw_pair():
        return remote(tw_part.at[1 - core], tw_sib, tws_send, tws_recv, sibling)

    pair_copy(1).start()
    tw_pair().start()
    z_sends(0)
    send_direct(MX + STEPS - 1)
    plane_sends(1)
    tw_pair().wait_recv()
    tw_sum[...] = (tw_part[core] + tw_sib[...]).astype(BF16)

    @pl.loop(1, ZL)
    def _(d):
        to = (lo + d) % ZL
        remote(
            tw_sum, tw_recv.at[lo], twz_send, twz_recv, (seq, to * NC + core)
        ).start()

    pltpu.make_async_copy(tw_sum, tw_recv.at[lo], twz_recv).start()
    forward(MX)
    z_sends(1)

    def gate(k):
        arrived(MX + k)
        gg_out[:, k] = (og_v[k].astype(F32) * in_buf[MX + k].astype(F32)).astype(BF16)

    @pl.loop(0, STEPS - 2)
    def _(k):
        forward(MX + k + 1)
        gate(k)

    gate(STEPS - 2)

    finish(0)
    drain(tw_recv, twz_recv)
    fin_v[2, core] = jnp.sum(tw_recv[...].astype(F32), axis=0) * scales[2]
    fin_copy(2).start()
    finish(1)
    gate(STEPS - 1)

    for m in range(3):
        fin_other(m).wait_recv()
    fin_out[...] = fin_v[...]

    @pl.loop(0, 4 * STEPS - 1)
    def _(i):
        across_copy(i).wait_send()
        drain(in_buf.at[i, pl.ds(0, PLANE - 1)], own_send.at[i])
        drain(in_buf.at[i, pl.ds(0, PLANE - 1)], fwd_send.at[i])

    last = 4 * STEPS - 1
    drain(in_buf.at[last, pl.ds(0, PLANE - 1)], own_send.at[last])
    drain(in_buf.at[last, pl.ds(0, PLANE)], direct_send)

    for m in range(2):
        pair_copy(m).wait_send()
        drain(plane_v.at[m, pl.ds(0, PLANE - 1)], pl_send.at[m])
        drain(zrecv_v.at[m, pl.ds(0, NZ - 1)], zz_send.at[m])
    tw_pair().wait_send()
    drain(tw_recv.at[pl.ds(0, ZL - 1)], twz_send)
    for m in range(3):
        fin_copy(m).wait_send()


def write_out(vg_in, gg_in, fin_in, vg, gg, two, one, tw, big_sem, fin_sem):
    part = SEQ // PARTS
    copies = [
        pltpu.make_async_copy(
            src.at[pl.ds(k * part, part)], dst.at[pl.ds(k * part, part)], big_sem.at[n, k]
        )
        for k in range(PARTS)
        for n, (src, dst) in enumerate(((vg_in, vg), (gg_in, gg)))
    ]
    copies += [
        pltpu.make_async_copy(
            fin_in.at[m, half], dst.at[:, pl.ds(half * 256, 256)], fin_sem.at[m, half]
        )
        for half in range(2)
        for m, dst in enumerate((two, one, tw))
    ]
    for copy in copies:
        copy.start()
    for copy in copies:
        copy.wait()


def body(seq_values, gate_values, out_grad, factor_one, factor_two, twiddle):
    width = seq_values.shape[0] * ZL * NC
    nblocks = factor_two.shape[0]
    block_len = factor_one.shape[0]
    scales = (
        1.0 / (width * block_len) ** 0.5,
        1.0 / (width * nblocks) ** 0.5,
        1.0 / width**0.5,
    )
    shape = (SEQ, STEPS, 16, 512)
    big = jax.ShapeDtypeStruct(shape, BF16)
    rows = jax.ShapeDtypeStruct((16, 512), F32)
    anywhere = pl.BlockSpec(memory_space=pl.ANY)
    per_step = (STEPS, SEQ, 16, 512)
    dma = pltpu.SemaphoreType.DMA
    items = 4 * STEPS
    kept = pl.pallas_call(
        functools.partial(kernel, scales),
        out_shape=(
            pltpu.VMEM(shape, BF16),
            pltpu.VMEM(shape, BF16),
            pltpu.VMEM((3, 2, 16, 256), F32),
        ),
        in_specs=[anywhere] * 6,
        out_specs=(pl.BlockSpec(memory_space=pltpu.VMEM),) * 3,
        scratch_shapes=[
            pltpu.VMEM(per_step, BF16),
            pltpu.VMEM(per_step, BF16),
            pltpu.VMEM(per_step, BF16),
            pltpu.VMEM((512, 512), BF16),
            pltpu.VMEM((512, 512), BF16),
            pltpu.VMEM((512, 512), BF16),
            pltpu.VMEM((16, 512), BF16),
            pltpu.VMEM(per_step, F32),
            pltpu.VMEM((items, SEQ, 16, 512), BF16),
            pltpu.VMEM((items - 1, PLANE, 16, 512), BF16),
            pltpu.VMEM((items, SEQ, 16, 512), BF16),
            pltpu.VMEM((2, 2, ZH, PLANE, 16, 256), F32),
            pltpu.VMEM((2, ZH, PLANE, 16, 256), F32),
            pltpu.VMEM((2, ZH, PLANE, 16, 256), F32),
            pltpu.VMEM((2, PLANE, ZH, 16, 256), F32),
            pltpu.VMEM((2, ZH, 16, 256), BF16),
            pltpu.VMEM((2, NZ, 16, 256), BF16),
            pltpu.VMEM((2, 16, 256), F32),
            pltpu.VMEM((16, 256), F32),
            pltpu.VMEM((16, 256), BF16),
            pltpu.VMEM((ZL, 16, 256), BF16),
            pltpu.VMEM((3, 2, 16, 256), F32),
            dma((3, STEPS)), dma((3,)),
            pltpu.SemaphoreType.REGULAR((5,)), pltpu.SemaphoreType.REGULAR,
            dma((items - 1,)), dma((items - 1,)), dma((items,)), dma((items - 1,)), dma((items,)),
            dma(()),
            dma((2,)), dma((2,)), dma((2,)), dma((2,)), dma((2,)), dma((2,)),
            dma(()), dma(()), dma(()), dma(()), dma((3,)), dma((3,)),
        ],
        compiler_params=pltpu.CompilerParams(
            collective_id=0, has_side_effects=True, vmem_limit_bytes=50 * 2**20
        ),
    )(
        seq_values.reshape(shape), gate_values.reshape(shape), out_grad.reshape(shape),
        factor_one, factor_two, twiddle,
    )
    vg, gg, two, one, tw = pl.pallas_call(
        write_out,
        out_shape=(big, big, rows, rows, rows),
        in_specs=[anywhere] * 3,
        out_specs=(anywhere,) * 5,
        scratch_shapes=[dma((2, PARTS)), dma((3, 2))],
        compiler_params=pltpu.CompilerParams(vmem_limit_bytes=4 * 2**20),
    )(*(pltpu.with_memory_space_constraint(part, pltpu.VMEM) for part in kept))
    whole = seq_values.shape
    return (vg.reshape(whole), gg.reshape(whole), one, two, tw)


def solution(mesh):
    return jax.shard_map(
        body,
        mesh=mesh,
        in_specs=(
            P("ch", "seq", None),
            P("ch", "seq", None),
            P("ch", "seq", None),
            P(),
            P(),
            P("seq", None),
        ),
        out_specs=(
            P("ch", "seq", None),
            P("ch", "seq", None),
            P("seq", None),
            P("seq", None),
            P("seq", None),
        ),
        check_vma=False,
    )
```

```python
import functools

import jax
import jax.numpy as jnp
from jax import lax
from jax.experimental import pallas as pl
from jax.experimental.pallas import tpu as pltpu
from jax.sharding import PartitionSpec as P

MESH = pl.DeviceIdType.MESH
NX, NY, ZH, ZL, NC = 4, 4, 2, 4, 2
PLANE = NX * NY
NZ = ZH * ZL
SEQ = ZH * PLANE
STEPS = 4
PARTS = 4
MG, MF, FG, MX = 0, STEPS, 2 * STEPS, 3 * STEPS
F32 = jnp.float32
BF16 = jnp.bfloat16


def dot(a, b, ca, cb):
    return lax.dot_general(a, b, (((ca,), (cb,)), ((), ())), preferred_element_type=F32)


def kernel(
    scales,
    x_hbm, gate_hbm, og_hbm, one_hbm, two_hbm, tw_hbm,
    vg_out, gg_out, fin_out,
    x_v, gate_v, og_v, one_v, two_v, two_t, tw_v, pre_v,
    out_buf, relay_buf, in_buf,
    grad_v, sib_v, sum_v, plane_v, zsend_v, zrecv_v,
    tw_part, tw_sib, tw_sum, tw_recv, fin_v,
    load_sem, mat_sem, round_sem, go_sem,
    z_send, z_recv, own_send, fwd_send, in_recv, direct_send,
    sib_send, sib_recv, pl_send, pl_recv, zz_send, zz_recv,
    tws_send, tws_recv, twz_send, twz_recv, fin_send, fin_recv,
):
    seq = lax.axis_index("seq")
    ch = lax.axis_index("ch")
    hi, at = seq // PLANE, seq % PLANE
    px, py = at // NY, at % NY
    lo, core = ch // NC, ch % NC
    z = hi * ZL + lo
    other_hi = 1 - hi

    def plane_at(d):
        return ((px + d // NY) % NX) * NY + (py + d % NY) % NY

    def plane_dev(to):
        return (hi * PLANE + to, ch)

    across = (other_hi * PLANE + at, ch)
    sibling = (seq, lo * NC + 1 - core)

    def z_dev(to):
        return ((to // ZL) * PLANE + at, (to % ZL) * NC + core)

    def remote(src, dst, ssem, rsem, dev):
        return pltpu.make_async_remote_copy(
            src_ref=src, dst_ref=dst, send_sem=ssem, recv_sem=rsem,
            device_id=dev, device_id_type=MESH,
        )

    def drain(ref, sem):
        pltpu.make_async_copy(ref, ref, sem).wait()

    def load(n, src, dst, k):
        return pltpu.make_async_copy(src.at[:, k], dst.at[k], load_sem.at[n, k])

    mats = (
        pltpu.make_async_copy(one_hbm, one_v, mat_sem.at[0]),
        pltpu.make_async_copy(tw_hbm, tw_v, mat_sem.at[1]),
        pltpu.make_async_copy(two_hbm, two_v, mat_sem.at[2]),
    )

    load(0, gate_hbm, gate_v, 0).start()
    load(1, og_hbm, og_v, 0).start()

    is_hub = (px % 2 == lo // 2) & (py % 2 == lo % 2) & (core == 0)

    def hub_at(h, bx, by, l):
        return (h * PLANE + (2 * bx + l // 2) * NY + 2 * by + l % 2, l * NC)

    bx, by = px // 2, py // 2
    my_hub = hub_at(hi, bx, by, lo)
    edges = (
        hub_at(hi, 1 - bx, by, lo),
        hub_at(hi, bx, 1 - by, lo),
        hub_at(hi, bx, by, lo + 1 - 2 * (lo % 2)),
        hub_at(hi, bx, by, (lo + 2) % ZL),
        across,
    )

    def member(j):
        mx = 2 * bx + (lo // 2 + j // 4) % 2
        my = 2 * by + (lo + j // 2) % 2
        return (hi * PLANE + mx * NY + my, lo * NC + j % 2)

    def tell(sem, dev):
        pl.semaphore_signal(sem, inc=1, device_id=dev, device_id_type=MESH)

    barrier = pltpu.get_barrier_semaphore()
    tell(barrier, across)

    @pl.when(is_hub)
    def _():
        for dev in edges[:-1]:
            tell(barrier, dev)

        @pl.loop(1, 8)
        def _(j):
            tell(barrier, member(j))

    @pl.when(jnp.logical_not(is_hub))
    def _():
        tell(barrier, my_hub)

    def enter():
        @pl.when(is_hub)
        def _():
            pl.semaphore_wait(barrier, 1 + len(edges) - 1 + 7)

        @pl.when(jnp.logical_not(is_hub))
        def _():
            pl.semaphore_wait(barrier, 2)

    def everyone_in():
        @pl.when(is_hub)
        def _():
            for n, dev in enumerate(edges):
                tell(round_sem.at[n], dev)
                pl.semaphore_wait(round_sem.at[n], 1)

            @pl.loop(1, 8)
            def _(j):
                tell(go_sem, member(j))

        @pl.when(jnp.logical_not(is_hub))
        def _():
            pl.semaphore_wait(go_sem, 1)

    for k in range(1, STEPS):
        load(0, gate_hbm, gate_v, k).start()
        load(1, og_hbm, og_v, k).start()
    mats[0].start()
    mats[1].start()
    for k in range(STEPS):
        load(2, x_hbm, x_v, k).start()
    mats[2].start()


    def across_copy(i):
        return remote(
            out_buf.at[i, pl.ds(other_hi * PLANE, PLANE)], relay_buf.at[i],
            z_send.at[i], z_recv.at[i], across,
        )

    def send_across(i):
        across_copy(i).start()

    def send_direct(i):
        @pl.loop(0, PLANE)
        def _(d):
            to = other_hi * PLANE + plane_at(d)
            remote(
                out_buf.at[i, to], in_buf.at[i, seq], direct_send, in_recv.at[i], (to, ch)
            ).start()

    def send_own(i):
        @pl.loop(1, PLANE)
        def _(d):
            to = plane_at(d)
            remote(
                out_buf.at[i, hi * PLANE + to], in_buf.at[i, seq],
                own_send.at[i], in_recv.at[i], plane_dev(to),
            ).start()

        pltpu.make_async_copy(out_buf.at[i, seq], in_buf.at[i, seq], in_recv.at[i]).start()

    def forward(i):
        across_copy(i).wait_recv()
        origin = other_hi * PLANE + at

        @pl.loop(1, PLANE)
        def _(d):
            to = plane_at(d)
            remote(
                relay_buf.at[i, to], in_buf.at[i, origin],
                fwd_send.at[i], in_recv.at[i], plane_dev(to),
            ).start()

        pltpu.make_async_copy(relay_buf.at[i, at], in_buf.at[i, origin], in_recv.at[i]).start()

    def arrived(i):
        drain(in_buf.at[i], in_recv.at[i])

    def flat(ref):
        return ref.reshape(SEQ * 16, 512)

    def blocks(value):
        return value.reshape(SEQ, 16, 512)

    def grad_at_home(k):
        load(0, gate_hbm, gate_v, k).wait()
        load(1, og_hbm, og_v, k).wait()
        out_buf[MG + k] = (gate_v[k].astype(F32) * og_v[k].astype(F32)).astype(BF16)

    grad_at_home(0)
    enter()
    send_across(MG)

    @pl.loop(1, STEPS)
    def _(k):
        grad_at_home(k)
        send_across(MG + k)

    mats[0].wait()
    mats[1].wait()

    @pl.loop(0, STEPS)
    def _(k):
        load(2, x_hbm, x_v, k).wait()
        pre = dot(x_v[k].reshape(SEQ * 16, 512), one_v[...], 1, 1)
        pre_v[k] = blocks(pre)
        out_buf[MF + k] = (blocks(pre) * tw_v[...].astype(F32)[None]).astype(BF16)
        send_across(MF + k)

    everyone_in()

    @pl.loop(MG, MF + STEPS)
    def _(i):
        send_own(i)

    mats[2].wait()
    two_t[...] = two_v[...].T
    grad_v[...] = jnp.zeros_like(grad_v)
    tw_part[...] = jnp.zeros_like(tw_part)
    forward(MG)

    @pl.loop(0, STEPS)
    def _(k):
        forward(MG + k + 1)
        arrived(MG + k)
        grad = in_buf[MG + k].reshape(SEQ * 16, 512)
        out_buf[FG + k] = blocks(dot(two_t[...], grad, 1, 0).astype(BF16))
        send_across(FG + k)
        send_own(FG + k)

    @pl.loop(0, STEPS)
    def _(k):
        forward(MF + k + 1)
        arrived(MF + k)
        first = in_buf[MF + k].reshape(SEQ * 16, 512)
        out_buf[MX + k] = blocks(dot(two_v[...], first, 1, 0).astype(BF16))

        @pl.when(k < STEPS - 1)
        def _():
            send_across(MX + k)

        send_own(MX + k)
        part = dot(in_buf[MG + k].reshape(SEQ * 16, 512), first, 1, 1)
        grad_v[0, 0] += part[:, :256].reshape(ZH, PLANE, 16, 256)
        grad_v[0, 1] += part[:, 256:].reshape(ZH, PLANE, 16, 256)

    def pair_copy(m):
        return remote(grad_v.at[m, 1 - core], sib_v.at[m], sib_send.at[m], sib_recv.at[m], sibling)

    def plane_sends(m):
        pair_copy(m).wait_recv()
        sum_v[m] = grad_v[m, core] + sib_v[m]

        @pl.loop(1, PLANE)
        def _(d):
            to = plane_at(d)
            remote(
                sum_v.at[m, :, to], plane_v.at[m, at],
                pl_send.at[m], pl_recv.at[m], plane_dev(to),
            ).start()

        pltpu.make_async_copy(sum_v.at[m, :, at], plane_v.at[m, at], pl_recv.at[m]).start()

    def z_sends(m):
        drain(plane_v.at[m], pl_recv.at[m])
        zsend_v[m] = jnp.sum(plane_v[m], axis=0).astype(BF16)

        @pl.loop(1, NZ)
        def _(d):
            to = (z + d) % NZ
            remote(
                zsend_v.at[m, to // ZL], zrecv_v.at[m, z],
                zz_send.at[m], zz_recv.at[m], z_dev(to),
            ).start()

        pltpu.make_async_copy(zsend_v.at[m, hi], zrecv_v.at[m, z], zz_recv.at[m]).start()

    def fin_copy(m):
        return remote(fin_v.at[m, core], fin_v.at[m, core], fin_send.at[m], fin_recv.at[m], sibling)

    def fin_other(m):
        return remote(
            fin_v.at[m, 1 - core], fin_v.at[m, 1 - core], fin_send.at[m], fin_recv.at[m], sibling
        )

    def finish(m):
        drain(zrecv_v.at[m], zz_recv.at[m])
        fin_v[m, core] = jnp.sum(zrecv_v[m].astype(F32), axis=0) * scales[m]
        fin_copy(m).start()

    pair_copy(0).start()
    plane_sends(0)

    @pl.loop(0, STEPS)
    def _(k):
        @pl.when(k < STEPS - 1)
        def _():
            forward(FG + k + 1)

        arrived(FG + k)
        fg = in_buf[FG + k].astype(F32)
        scaled = (fg * tw_v[...].astype(F32)[None]).astype(BF16)
        tw_add = jnp.sum(fg * pre_v[k], axis=0)
        tw_part[0] += tw_add[:, :256]
        tw_part[1] += tw_add[:, 256:]
        scaled = scaled.reshape(SEQ * 16, 512)
        vg_out[:, k] = blocks(dot(scaled, one_v[...], 1, 0).astype(BF16))
        part = dot(scaled, x_v[k].reshape(SEQ * 16, 512), 0, 0)
        grad_v[1, 0] += part[:, :256].reshape(ZH, PLANE, 16, 256)
        grad_v[1, 1] += part[:, 256:].reshape(ZH, PLANE, 16, 256)

    def tw_pair():
        return remote(tw_part.at[1 - core], tw_sib, tws_send, tws_recv, sibling)

    pair_copy(1).start()
    tw_pair().start()
    z_sends(0)
    send_direct(MX + STEPS - 1)
    plane_sends(1)
    tw_pair().wait_recv()
    tw_sum[...] = (tw_part[core] + tw_sib[...]).astype(BF16)

    @pl.loop(1, ZL)
    def _(d):
        to = (lo + d) % ZL
        remote(
            tw_sum, tw_recv.at[lo], twz_send, twz_recv, (seq, to * NC + core)
        ).start()

    pltpu.make_async_copy(tw_sum, tw_recv.at[lo], twz_recv).start()
    forward(MX)
    z_sends(1)

    def gate(k):
        arrived(MX + k)
        gg_out[:, k] = (og_v[k].astype(F32) * in_buf[MX + k].astype(F32)).astype(BF16)

    @pl.loop(0, STEPS - 2)
    def _(k):
        forward(MX + k + 1)
        gate(k)

    def sent(i):
        across_copy(i).wait_send()
        drain(in_buf.at[i, pl.ds(0, PLANE - 1)], own_send.at[i])
        drain(in_buf.at[i, pl.ds(0, PLANE - 1)], fwd_send.at[i])

    @pl.loop(0, MX + STEPS - 2)
    def _(i):
        sent(i)

    for m in range(2):
        pair_copy(m).wait_send()
        drain(plane_v.at[m, pl.ds(0, PLANE - 1)], pl_send.at[m])
    drain(zrecv_v.at[0, pl.ds(0, NZ - 1)], zz_send.at[0])
    tw_pair().wait_send()

    gate(STEPS - 2)

    finish(0)
    drain(tw_recv, twz_recv)
    fin_v[2, core] = jnp.sum(tw_recv[...].astype(F32), axis=0) * scales[2]
    fin_copy(2).start()
    finish(1)
    gate(STEPS - 1)

    for m in range(3):
        fin_other(m).wait_recv()
    fin_out[...] = fin_v[...]

    sent(MX + STEPS - 2)
    last = 4 * STEPS - 1
    drain(in_buf.at[last, pl.ds(0, PLANE - 1)], own_send.at[last])
    drain(in_buf.at[last, pl.ds(0, PLANE)], direct_send)

    drain(zrecv_v.at[1, pl.ds(0, NZ - 1)], zz_send.at[1])
    drain(tw_recv.at[pl.ds(0, ZL - 1)], twz_send)
    for m in range(3):
        fin_copy(m).wait_send()


def write_out(vg_in, gg_in, fin_in, vg, gg, two, one, tw, big_sem, fin_sem):
    part = SEQ // PARTS
    copies = [
        pltpu.make_async_copy(
            src.at[pl.ds(k * part, part)], dst.at[pl.ds(k * part, part)], big_sem.at[n, k]
        )
        for k in range(PARTS)
        for n, (src, dst) in enumerate(((vg_in, vg), (gg_in, gg)))
    ]
    copies += [
        pltpu.make_async_copy(
            fin_in.at[m, half], dst.at[:, pl.ds(half * 256, 256)], fin_sem.at[m, half]
        )
        for half in range(2)
        for m, dst in enumerate((two, one, tw))
    ]
    for copy in copies:
        copy.start()
    for copy in copies:
        copy.wait()


def body(seq_values, gate_values, out_grad, factor_one, factor_two, twiddle):
    width = seq_values.shape[0] * ZL * NC
    nblocks = factor_two.shape[0]
    block_len = factor_one.shape[0]
    scales = (
        1.0 / (width * block_len) ** 0.5,
        1.0 / (width * nblocks) ** 0.5,
        1.0 / width**0.5,
    )
    shape = (SEQ, STEPS, 16, 512)
    big = jax.ShapeDtypeStruct(shape, BF16)
    rows = jax.ShapeDtypeStruct((16, 512), F32)
    anywhere = pl.BlockSpec(memory_space=pl.ANY)
    per_step = (STEPS, SEQ, 16, 512)
    dma = pltpu.SemaphoreType.DMA
    items = 4 * STEPS
    kept = pl.pallas_call(
        functools.partial(kernel, scales),
        out_shape=(
            pltpu.VMEM(shape, BF16),
            pltpu.VMEM(shape, BF16),
            pltpu.VMEM((3, 2, 16, 256), F32),
        ),
        in_specs=[anywhere] * 6,
        out_specs=(pl.BlockSpec(memory_space=pltpu.VMEM),) * 3,
        scratch_shapes=[
            pltpu.VMEM(per_step, BF16),
            pltpu.VMEM(per_step, BF16),
            pltpu.VMEM(per_step, BF16),
            pltpu.VMEM((512, 512), BF16),
            pltpu.VMEM((512, 512), BF16),
            pltpu.VMEM((512, 512), BF16),
            pltpu.VMEM((16, 512), BF16),
            pltpu.VMEM(per_step, F32),
            pltpu.VMEM((items, SEQ, 16, 512), BF16),
            pltpu.VMEM((items - 1, PLANE, 16, 512), BF16),
            pltpu.VMEM((items, SEQ, 16, 512), BF16),
            pltpu.VMEM((2, 2, ZH, PLANE, 16, 256), F32),
            pltpu.VMEM((2, ZH, PLANE, 16, 256), F32),
            pltpu.VMEM((2, ZH, PLANE, 16, 256), F32),
            pltpu.VMEM((2, PLANE, ZH, 16, 256), F32),
            pltpu.VMEM((2, ZH, 16, 256), BF16),
            pltpu.VMEM((2, NZ, 16, 256), BF16),
            pltpu.VMEM((2, 16, 256), F32),
            pltpu.VMEM((16, 256), F32),
            pltpu.VMEM((16, 256), BF16),
            pltpu.VMEM((ZL, 16, 256), BF16),
            pltpu.VMEM((3, 2, 16, 256), F32),
            dma((3, STEPS)), dma((3,)),
            pltpu.SemaphoreType.REGULAR((5,)), pltpu.SemaphoreType.REGULAR,
            dma((items - 1,)), dma((items - 1,)), dma((items,)), dma((items - 1,)), dma((items,)),
            dma(()),
            dma((2,)), dma((2,)), dma((2,)), dma((2,)), dma((2,)), dma((2,)),
            dma(()), dma(()), dma(()), dma(()), dma((3,)), dma((3,)),
        ],
        compiler_params=pltpu.CompilerParams(
            collective_id=0, has_side_effects=True, vmem_limit_bytes=50 * 2**20
        ),
    )(
        seq_values.reshape(shape), gate_values.reshape(shape), out_grad.reshape(shape),
        factor_one, factor_two, twiddle,
    )
    vg, gg, two, one, tw = pl.pallas_call(
        write_out,
        out_shape=(big, big, rows, rows, rows),
        in_specs=[anywhere] * 3,
        out_specs=(anywhere,) * 5,
        scratch_shapes=[dma((2, PARTS)), dma((3, 2))],
        compiler_params=pltpu.CompilerParams(vmem_limit_bytes=4 * 2**20),
    )(*(pltpu.with_memory_space_constraint(part, pltpu.VMEM) for part in kept))
    whole = seq_values.shape
    return (vg.reshape(whole), gg.reshape(whole), one, two, tw)


def solution(mesh):
    return jax.shard_map(
        body,
        mesh=mesh,
        in_specs=(
            P("ch", "seq", None),
            P("ch", "seq", None),
            P("ch", "seq", None),
            P(),
            P(),
            P("seq", None),
        ),
        out_specs=(
            P("ch", "seq", None),
            P("ch", "seq", None),
            P("seq", None),
            P("seq", None),
            P("seq", None),
        ),
        check_vma=False,
    )
```
